256 devices in a mesh: replica: 8 (over y_lo, x), fsdp: 32 (over z, y_hi, core).
Axes of the slice: x: 4, y: 4 (y_hi: 2, y_lo: 2; y = y_hi * 2 + y_lo), z: 8, core: 2. Of those that a mesh axis runs over, the one named last changes fastest.
Arguments:
- tokens: bfloat16 [98304, 4608], P(('replica', 'fsdp')), may hold values from -6 to 6
- key_weight: bfloat16 [8, 4608, 1024], P('replica', 'fsdp'), may hold values from -0.09375 to 0.09375
- key_cotangent: bfloat16 [98304, 1024], P(('replica', 'fsdp')), may hold values from -6 to 6
- fragment: float32 [512, 4096], P('fsdp'), may hold values from -6 to 6
- momentum: float32 [512, 4096], P('fsdp'), may hold values from -6 to 6
- pseudo_grad: float32 [8, 512, 4096], P('replica', 'fsdp'), may hold values from -6 to 6
- sign_flips: int32 [512, 4096], P('fsdp'), may hold values from -1 to 1, as said below
- kept_rows: int32 [512, 512], P('fsdp'), may hold values from 0 to 4095, as said below
Outputs:
- projected: bfloat16 [98304, 1024], P(('replica', 'fsdp'))
- token_grad: bfloat16 [98304, 4608], P(('replica', 'fsdp'))
- weight_grad: bfloat16 [8, 4608, 1024], P('replica', 'fsdp')
- new_fragment: float32 [512, 4096], P('fsdp')
- new_momentum: float32 [512, 4096], P('fsdp')
The draws below stay inside these ranges and needn't reach their ends.
Inputs may be any that keep to these rules, and one draw needn't show every extreme that they name: `sign_flips`: every entry is -1 or 1. `kept_rows`: each row holds 512 different column numbers of a block, in increasing order.
All inputs are finite; a program needn't handle non-finite values.
Results may differ from the reference program's by a relative error of at most 0.02.
Values may be sent and summed in bfloat16 or wider, within the bound.
No kernel may reach another device: no remote copies, remote signals or barrier semaphores. Data moves between devices by JAX's collectives and lax.ppermute only.
A program may use at most 128 MiB of HBM per device.

```python
import jax
import jax.numpy as jnp
from jax import lax

D = 4608
TOK_DEV = 384
SIDE = 64
KV_WIDTH = 1024
REPLICAS = 8
TOKENS = 98304
BLOCK = 4096
KEEP = 512
FBLOCKS = 512
N_REPLICA = 8
N_FSDP = 32


def draw_sign_flips(key, part):
    key = jax.random.fold_in(key, 11)
    coins = jax.random.randint(key, (FBLOCKS, BLOCK), 0, 2)
    return (2 * coins - 1).astype(jnp.int32)


def draw_kept_rows(key, part):
    key = jax.random.fold_in(key, 23)
    first_key = jax.random.fold_in(key, 5)
    row_keys = jax.random.split(key, FBLOCKS)

    def subset_of(row_key):
        order = jax.random.permutation(row_key, BLOCK)
        return jnp.sort(order[:KEEP])
    chosen = jax.vmap(subset_of)(row_keys).astype(jnp.int32)
    inner = jax.random.permutation(first_key, BLOCK - 2)[:KEEP - 2] + 1
    ends = jnp.array([0, BLOCK - 1], jnp.int32)
    first_row = jnp.sort(jnp.concatenate([ends, inner.astype(jnp.int32)]))
    return chosen.at[0].set(first_row).astype(jnp.int32)


def block_scale(own_key, shape, cuts, smallest, largest):
    def one(dim, shards_of):
        heights = jax.random.uniform(jax.random.fold_in(jax.random.fold_in(own_key, 6), dim), (shards_of,), jnp.float32, smallest / len(cuts), largest / len(cuts))
        return jnp.repeat(jnp.exp(heights), shape[dim] // shards_of).reshape((-1,) + (1,) * (len(shape) - dim - 1))

    loudness = one(*cuts[0])
    for cut in cuts[1:]:
        loudness = loudness * one(*cut)
    return loudness


def centred(key, shape, scale, bound, shards=(), held_as=jnp.bfloat16):
    values = jax.random.normal(key, shape, jnp.float32) * scale
    if len(shards) > 0:
        values = block_scale(key, shape, shards, -0.22, 0.18) * values
    return jnp.clip(values, min=-bound, max=bound).astype(held_as)


def setup_inputs(seed: int = 0) -> dict:
    key_list = jax.random.split(jax.random.key(seed), 9)
    tokens = centred(key_list[0], (TOKENS, D), 1.0, 6.0, ((0, 256),))
    key_weight = centred(key_list[1], (REPLICAS, D, KV_WIDTH), D ** -0.5, 0.09375, ((0, 8), (1, 32)))
    key_cotangent = centred(key_list[2], (TOKENS, KV_WIDTH), 1.0, 6.0, ((0, 256),))
    fragment = centred(key_list[3], (FBLOCKS, BLOCK), 1.0, 6.0, ((0, 32),), jnp.float32)
    momentum = centred(key_list[4], (FBLOCKS, BLOCK), 1.0, 6.0, ((0, 32),), jnp.float32)
    pseudo_grad = centred(key_list[5], (REPLICAS, FBLOCKS, BLOCK), 1.0, 6.0, ((0, 8), (1, 32)), jnp.float32)
    sign_flips = draw_sign_flips(jax.random.fold_in(key_list[8], 71), 0)
    kept_rows = draw_kept_rows(jax.random.fold_in(key_list[8], 71), 0)
    return {"tokens": tokens, "key_weight": key_weight, "key_cotangent": key_cotangent, "fragment": fragment, "momentum": momentum, "pseudo_grad": pseudo_grad, "sign_flips": sign_flips, "kept_rows": kept_rows}


def sylvester(extent):
    row_index = lax.broadcasted_iota(jnp.int32, (extent, extent), 0)
    col_index = lax.broadcasted_iota(jnp.int32, (extent, extent), 1)
    common = jnp.bitwise_and(row_index, col_index)
    parity = jnp.zeros((extent, extent), jnp.int32)
    for position in range(extent.bit_length()):
        parity = parity + jnp.bitwise_and(jnp.right_shift(common, position), 1)
    return (1 - 2 * (parity % 2)).astype(jnp.float32)


def transform(values, hadamard, extent):
    count_rows = values.shape[0]
    shaped = values.reshape(count_rows, extent, extent)
    first = jnp.einsum('nij,ai->naj', shaped, hadamard, precision=lax.Precision.HIGHEST)
    second = jnp.einsum('naj,bj->nab', first, hadamard, precision=lax.Precision.HIGHEST)
    return second.reshape(count_rows, extent * extent) / extent


def reference(tokens, key_weight, key_cotangent, fragment, momentum, pseudo_grad, sign_flips, kept_rows):
    scaling = (TOK_DEV * N_FSDP) ** -0.5
    tok_groups = tokens.reshape(N_REPLICA, N_FSDP, TOK_DEV, D)
    cot_groups = key_cotangent.reshape(N_REPLICA, N_FSDP, TOK_DEV, KV_WIDTH)

    def group_step(operands):
        group_tokens, group_cot, weights = operands
        flat_tokens = group_tokens.reshape(N_FSDP * TOK_DEV, D)
        flat_cot = group_cot.reshape(N_FSDP * TOK_DEV, KV_WIDTH)
        keys_group = jnp.dot(flat_tokens, weights, preferred_element_type=jnp.float32).astype(jnp.bfloat16)
        grad_group = jnp.dot(flat_cot, weights.T, preferred_element_type=jnp.float32).astype(jnp.bfloat16)

        def add_run(running, run_pair):
            run_tokens, run_cot = run_pair
            term = (jnp.dot(run_tokens.T, run_cot, preferred_element_type=jnp.float32) * scaling).astype(jnp.bfloat16)
            term = lax.optimization_barrier(term)
            return running + term.astype(jnp.float32), None

        summed, ignored = lax.scan(add_run, jnp.zeros((D, KV_WIDTH), jnp.float32), (group_tokens, group_cot))
        return keys_group, grad_group, summed.astype(jnp.bfloat16)

    keys_all, grads_all, weight_grad = lax.map(group_step, (tok_groups, cot_groups, key_weight))
    projected = keys_all.reshape(TOKENS, KV_WIDTH)
    token_grad = grads_all.reshape(TOKENS, D)

    hadamard = sylvester(SIDE)
    signs_float = sign_flips.astype(jnp.float32)
    flipped = signs_float[None] * pseudo_grad
    spread = transform(flipped.reshape(N_REPLICA * FBLOCKS, BLOCK), hadamard, SIDE).reshape(N_REPLICA, FBLOCKS, BLOCK)
    chosen = jnp.broadcast_to(kept_rows[None], (N_REPLICA, FBLOCKS, KEEP))
    sketches = jnp.take_along_axis(spread, chosen, axis=2)
    mean_sketch = jnp.sum(sketches, axis=0) / N_REPLICA
    row_ids = lax.broadcasted_iota(jnp.int32, (FBLOCKS, KEEP), 0)
    placed = jnp.zeros((FBLOCKS, BLOCK), jnp.float32).at[row_ids, kept_rows].set(mean_sketch)
    estimate = (BLOCK / KEEP) * signs_float * transform(placed, hadamard, SIDE)
    new_momentum = 0.9 * momentum + estimate
    new_fragment = fragment - 0.7 * (estimate + 0.9 * new_momentum)
    return projected, token_grad, weight_grad, new_fragment, new_momentum
```

```python
import jax
import jax.numpy as jnp
from jax import lax
from jax.experimental import pallas as pl
from jax.experimental.pallas import tpu as pltpu
from jax.sharding import PartitionSpec as P

LANES = 128
STEP = 512
VMEM_LIMIT = 48 * 1024 * 1024
SMALL = pl.CostEstimate(flops=1024, bytes_accessed=1024, transcendentals=0)
Z_WAYS = 8
X_WAYS = 4


def sylvester(extent):
    row_index = lax.broadcasted_iota(jnp.int32, (extent, extent), 0)
    col_index = lax.broadcasted_iota(jnp.int32, (extent, extent), 1)
    common = jnp.bitwise_and(row_index, col_index)
    parity = jnp.zeros((extent, extent), jnp.int32)
    for position in range(extent.bit_length()):
        parity = parity + jnp.bitwise_and(jnp.right_shift(common, position), 1)
    return (1 - 2 * jnp.bitwise_and(parity, 1)).astype(jnp.float32)


def in_three(values):
    high = values.astype(jnp.bfloat16)
    rest = values - high.astype(jnp.float32)
    middle = rest.astype(jnp.bfloat16)
    low = (rest - middle.astype(jnp.float32)).astype(jnp.bfloat16)
    return high, middle, low


def transform(tiles):
    tiles = list(tiles)
    distance = 1
    while distance < len(tiles):
        for at in range(len(tiles)):
            if at & distance == 0:
                low, high = tiles[at], tiles[at + distance]
                tiles[at], tiles[at + distance] = low + high, low - high
        distance *= 2
    rows = tiles[0].shape[0]
    stacked = jnp.concatenate(tiles, axis=0)
    signs = sylvester(LANES).astype(jnp.bfloat16)
    product = sum(
        jnp.dot(part, signs, preferred_element_type=jnp.float32) for part in in_three(stacked)
    )
    return [product[at * rows : (at + 1) * rows] for at in range(len(tiles))]


def sketch_of(pseudo_grad, sign_flips, kept_rows):
    rows, block = pseudo_grad.shape
    keep = kept_rows.shape[1]
    count = block // LANES

    def kernel(grad_ref, signs_ref, kept_ref, out_ref):
        tiles = []
        for at in range(count):
            lanes = slice(at * LANES, (at + 1) * LANES)
            tiles.append(grad_ref[:, lanes] * signs_ref[:, lanes].astype(jnp.float32))
        spread = transform(tiles)
        for at in range(keep // LANES):
            lanes = slice(at * LANES, (at + 1) * LANES)
            kept = kept_ref[:, lanes]
            column = jnp.bitwise_and(kept, LANES - 1)
            tile = jnp.right_shift(kept, LANES.bit_length() - 1)
            picked = jnp.zeros((rows, LANES), jnp.float32)
            for other in range(count):
                values = jnp.take_along_axis(spread[other], column, axis=1)
                picked = jnp.where(tile == other, values, picked)
            out_ref[:, lanes] = picked * (block**-0.5)

    return pl.pallas_call(
        kernel,
        out_shape=jax.ShapeDtypeStruct((rows, keep), jnp.float32),
        in_specs=[pl.BlockSpec(memory_space=pltpu.VMEM)] * 3,
        out_specs=pl.BlockSpec(memory_space=pltpu.VMEM),
        compiler_params=pltpu.CompilerParams(vmem_limit_bytes=VMEM_LIMIT),
        cost_estimate=SMALL,
    )(pseudo_grad, sign_flips, kept_rows)


def outer_step(total, groups, kept_rows, sign_flips, momentum, fragment):
    rows, block = fragment.shape
    keep = kept_rows.shape[1]
    count = block // LANES
    scale = (block / keep) * block**-0.5

    def kernel(total_ref, kept_ref, signs_ref, momentum_ref, fragment_ref, *refs):
        fragment_out, momentum_out, placed = refs
        mean = total_ref[...] * (1.0 / groups)
        column = jnp.bitwise_and(kept_ref[...], LANES - 1)
        tile = jnp.right_shift(kept_ref[...], LANES.bit_length() - 1)
        tile_index = lax.broadcasted_iota(jnp.int32, (count, keep), 0)
        column_index = lax.broadcasted_iota(jnp.int32, (LANES, keep), 0)
        for row in range(rows):
            this = slice(row, row + 1)
            spots = jnp.where(tile[this] == tile_index, mean[this], 0.0)
            lines = jnp.where(column[this] == column_index, 1.0, 0.0).astype(jnp.bfloat16)
            sums = lax.dot_general(
                jnp.concatenate(in_three(spots), axis=0),
                lines,
                (((1,), (1,)), ((), ())),
                preferred_element_type=jnp.float32,
            )
            placed[row] = sums[:count] + sums[count : 2 * count] + sums[2 * count :]
        spread = transform([placed[:, at, :] for at in range(count)])
        for at in range(count):
            lanes = slice(at * LANES, (at + 1) * LANES)
            estimate = scale * signs_ref[:, lanes].astype(jnp.float32) * spread[at]
            momentum_now = 0.9 * momentum_ref[:, lanes] + estimate
            momentum_out[:, lanes] = momentum_now
            fragment_out[:, lanes] = fragment_ref[:, lanes] - 0.7 * (estimate + 0.9 * momentum_now)

    return pl.pallas_call(
        kernel,
        out_shape=[jax.ShapeDtypeStruct((rows, block), jnp.float32)] * 2,
        in_specs=[pl.BlockSpec(memory_space=pltpu.VMEM)] * 5,
        out_specs=[pl.BlockSpec(memory_space=pltpu.VMEM)] * 2,
        scratch_shapes=[pltpu.VMEM((rows, count, LANES), jnp.float32)],
        compiler_params=pltpu.CompilerParams(vmem_limit_bytes=VMEM_LIMIT),
        cost_estimate=SMALL,
    )(total, kept_rows, sign_flips, momentum, fragment)


def index_of(z, column, core):
    return z * 4 + column * 2 + core


def places():
    return [(z, y, c) for z in range(Z_WAYS) for y in range(2) for c in range(2)]


RING = [
    (index_of(z, y, c), index_of((z + 1 - 2 * c) % Z_WAYS, y, c)) for z, y, c in places()
]
COLUMN = [(index_of(z, y, c), index_of(z, 1 - y, c)) for z, y, c in places()]
CORE = [(index_of(z, y, c), index_of(z, y, 1 - c)) for z, y, c in places()]


def ring(block):
    return lax.ppermute(block, "fsdp", RING)


def across(block):
    return lax.ppermute(block, "fsdp", COLUMN)


def twin(block):
    return lax.ppermute(block, "fsdp", CORE)


def replica_sum(sketch):
    total = sketch
    for distance in (1, 2, X_WAYS):
        pairs = [(at, at ^ distance) for at in range(2 * X_WAYS)]
        total = total + lax.ppermute(total, "replica", pairs)
    return total


def term_pieces(tokens, cotangent, scaling, starts, counts, rows):
    depth, width = tokens.shape[1], cotangent.shape[1]
    total = sum(counts)

    def kernel(starts_ref, tokens_ref, cotangent_ref, *refs):
        outs, (term, sems) = refs[: len(counts)], refs[len(counts) :]
        for at in range(0, depth, STEP):
            part = lax.dot_general(
                tokens_ref[:, at : at + STEP],
                cotangent_ref[...],
                (((0,), (0,)), ((), ())),
                preferred_element_type=jnp.float32,
            )
            term[at : at + STEP, :] = (part * scaling).astype(term.dtype)
        copies = []
        for out, count in zip(outs, counts):
            for part in range(count):
                start = pl.multiple_of(starts_ref[len(copies)], 16)
                copies.append(
                    pltpu.make_async_copy(
                        term.at[pl.ds(start, rows), :],
                        out.at[pl.ds(part * rows, rows), :],
                        sems.at[len(copies)],
                    )
                )
        for copy in copies:
            copy.start()
        for copy in copies:
            copy.wait()

    return pl.pallas_call(
        kernel,
        out_shape=[jax.ShapeDtypeStruct((count * rows, width), jnp.bfloat16) for count in counts],
        in_specs=[pl.BlockSpec(memory_space=pltpu.SMEM)]
        + [pl.BlockSpec(memory_space=pltpu.VMEM)] * 2,
        out_specs=[pl.BlockSpec(memory_space=pl.ANY)] * len(counts),
        scratch_shapes=[
            pltpu.VMEM((depth, width), jnp.bfloat16),
            pltpu.SemaphoreType.DMA((total,)),
        ],
        compiler_params=pltpu.CompilerParams(vmem_limit_bytes=VMEM_LIMIT),
        cost_estimate=SMALL,
    )(starts, tokens, cotangent)


def project(tokens, cotangent, pieces, starts, rows):
    count, depth, width = tokens.shape[0], tokens.shape[1], cotangent.shape[1]
    total = sum(piece.shape[0] // rows for piece in pieces)

    def kernel(starts_ref, tokens_ref, cotangent_ref, *refs):
        sources = refs[: len(pieces)]
        projected, token_grad, weight, sems = refs[len(pieces) :]
        copies = []
        for source in sources:
            for part in range(source.shape[0] // rows):
                start = pl.multiple_of(starts_ref[len(copies)], 16)
                copies.append(
                    pltpu.make_async_copy(
                        source.at[pl.ds(part * rows, rows), :],
                        weight.at[pl.ds(start, rows), :],
                        sems.at[len(copies)],
                    )
                )
        for copy in copies:
            copy.start()
        for copy in copies:
            copy.wait()
        for at in range(0, depth, STEP):
            token_grad[:, at : at + STEP] = lax.dot_general(
                cotangent_ref[...],
                weight[at : at + STEP, :],
                (((1,), (1,)), ((), ())),
                preferred_element_type=jnp.float32,
            ).astype(token_grad.dtype)
        for at in range(0, width, STEP // 2):
            projected[:, at : at + STEP // 2] = jnp.dot(
                tokens_ref[...],
                weight[:, at : at + STEP // 2],
                preferred_element_type=jnp.float32,
            ).astype(projected.dtype)

    return pl.pallas_call(
        kernel,
        out_shape=[
            jax.ShapeDtypeStruct((count, width), jnp.bfloat16),
            jax.ShapeDtypeStruct((count, depth), jnp.bfloat16),
        ],
        in_specs=[pl.BlockSpec(memory_space=pltpu.SMEM)]
        + [pl.BlockSpec(memory_space=pltpu.VMEM)] * 2
        + [pl.BlockSpec(memory_space=pl.ANY)] * len(pieces),
        out_specs=[pl.BlockSpec(memory_space=pltpu.VMEM)] * 2,
        scratch_shapes=[
            pltpu.VMEM((depth, width), jnp.bfloat16),
            pltpu.SemaphoreType.DMA((total,)),
        ],
        compiler_params=pltpu.CompilerParams(vmem_limit_bytes=VMEM_LIMIT),
        cost_estimate=SMALL,
    )(starts, tokens, cotangent, *pieces)


def join(first, second):
    rows, width = first.shape

    def kernel(first_ref, second_ref, out_ref):
        out_ref[:rows, :] = first_ref[...]
        out_ref[rows:, :] = second_ref[...]

    return pl.pallas_call(
        kernel,
        out_shape=jax.ShapeDtypeStruct((2 * rows, width), first.dtype),
        in_specs=[pl.BlockSpec(memory_space=pltpu.VMEM)] * 2,
        out_specs=pl.BlockSpec(memory_space=pltpu.VMEM),
        cost_estimate=SMALL,
    )(first, second)


def local(
    tokens, key_weight, key_cotangent, fragment, momentum, pseudo_grad, sign_flips, kept_rows
):
    own = key_weight[0]
    rows, width = own.shape
    fsdp_ways = lax.axis_size("fsdp")
    place = lax.axis_index("fsdp")
    z, column, core = place // 4, (place // 2) % 2, place % 2
    other, mate = 1 - column, 1 - core
    ahead = 1 - 2 * core
    scaling = (tokens.shape[0] * fsdp_ways) ** (-0.5)
    wide, narrow = jnp.float32, jnp.bfloat16

    def row_of(distance, at_column, at_core):
        return index_of((z + distance) % Z_WAYS, at_column, at_core) * rows

    own_twin = twin(own)
    side = across(own)
    side_twin = twin(side)
    first, second = [join(own, own_twin)], [join(side, side_twin)]
    tokens, first[0] = lax.optimization_barrier((tokens, first[0]))
    for step in range(3):
        first.append(ring(first[-1]))
        second.append(ring(second[-1]))
    last = ring(jnp.where(core == 0, first[3], second[3]))
    pieces, starts = [own, own_twin, side, side_twin], [
        row_of(0, column, core),
        row_of(0, column, mate),
        row_of(0, other, core),
        row_of(0, other, mate),
    ]

    def share(block, distance, at_column, twin_column):
        pieces.extend([block, twin(block)])
        starts.extend([row_of(-ahead * distance, at_column, at) for at in (core, mate)])
        starts.extend([row_of(ahead * distance, twin_column, at) for at in (mate, core)])

    for step in range(1, 4):
        share(first[step], step, column, column)
        share(second[step], step, other, other)
    share(last, 4, jnp.where(core == 0, column, other), jnp.where(core == 0, other, column))
    starts = jnp.stack(starts).astype(jnp.int32)

    counts, rows_of = [], []
    for far in (4, 3, 2, 1, 0):
        halves = ((core,), (mate,)) if far in (0, 4) else ((core, mate), (mate, core))
        for sign, half in zip((1, -1), halves):
            rows_of += [
                row_of(sign * ahead * far, at_column, at) for at_column in (column, other) for at in half
            ]
            counts.append(2 * len(half))
    parts = term_pieces(
        tokens, key_cotangent, scaling, jnp.stack(rows_of).astype(jnp.int32), counts, rows
    )
    mine, got = parts[0::2], [twin(part) for part in parts[1::2]]

    def own_sum(at):
        extent = mine[at].shape[0] // 2
        return mine[at][:extent].astype(wide) + got[at][:extent].astype(wide)

    over = []
    for at in range(5):
        extent = mine[at].shape[0] // 2
        over.append(
            across((mine[at][extent:].astype(wide) + got[at][extent:].astype(wide)).astype(narrow))
        )
    come = ring((own_sum(0) + over[0].astype(wide)).astype(narrow)).astype(wide)
    total = own_sum(1) + over[1].astype(wide) + jnp.pad(come, ((0, rows), (0, 0)))
    come = ring(total.astype(narrow)).astype(wide)
    come = ring((own_sum(2) + over[2].astype(wide) + come).astype(narrow)).astype(wide)
    come = ring((own_sum(3) + over[3].astype(wide) + come).astype(narrow))
    rest = twin(come[rows:])
    weight_grad = (
        own_sum(4) + over[4].astype(wide) + come[:rows].astype(wide) + rest.astype(wide)
    ).astype(narrow)[None]

    local_sketch = sketch_of(pseudo_grad[0], sign_flips, kept_rows)
    new_fragment, new_momentum = outer_step(
        replica_sum(local_sketch),
        lax.axis_size("replica"),
        kept_rows,
        sign_flips,
        momentum,
        fragment,
    )

    projected, token_grad = project(tokens, key_cotangent, pieces, starts, rows)
    return (projected, token_grad, weight_grad, new_fragment, new_momentum)


def solution(mesh):
    placed = (
        P(("replica", "fsdp"), None),
        P("replica", "fsdp", None),
        P(("replica", "fsdp"), None),
        P("fsdp", None),
        P("fsdp", None),
        P("replica", "fsdp", None),
        P("fsdp", None),
        P("fsdp", None),
    )
    return jax.shard_map(
        local,
        mesh=mesh,
        in_specs=placed,
        out_specs=(
            P(("replica", "fsdp"), None),
            P(("replica", "fsdp"), None),
            P("replica", "fsdp", None),
            P("fsdp", None),
            P("fsdp", None),
        ),
        check_vma=False,
    )
```

```python
import jax
import jax.numpy as jnp
from jax import lax
from jax.experimental import pallas as pl
from jax.experimental.pallas import tpu as pltpu
from jax.sharding import PartitionSpec as P

LANES = 128
STEP = 512
MIB = 1024 * 1024
LARGE = 60 * MIB
SMALL = pl.CostEstimate(flops=1024, bytes_accessed=1024, transcendentals=0)
Z_WAYS = 8
X_WAYS = 4


def sylvester(extent):
    row_index = lax.broadcasted_iota(jnp.int32, (extent, extent), 0)
    col_index = lax.broadcasted_iota(jnp.int32, (extent, extent), 1)
    common = jnp.bitwise_and(row_index, col_index)
    parity = jnp.zeros((extent, extent), jnp.int32)
    for position in range(extent.bit_length()):
        parity = parity + jnp.bitwise_and(jnp.right_shift(common, position), 1)
    return (1 - 2 * jnp.bitwise_and(parity, 1)).astype(jnp.float32)


def in_three(values):
    high = values.astype(jnp.bfloat16)
    rest = values - high.astype(jnp.float32)
    middle = rest.astype(jnp.bfloat16)
    low = (rest - middle.astype(jnp.float32)).astype(jnp.bfloat16)
    return high, middle, low


def transform(tiles):
    tiles = list(tiles)
    distance = 1
    while distance < len(tiles):
        for at in range(len(tiles)):
            if at & distance == 0:
                low, high = tiles[at], tiles[at + distance]
                tiles[at], tiles[at + distance] = low + high, low - high
        distance *= 2
    rows = tiles[0].shape[0]
    stacked = jnp.concatenate(tiles, axis=0)
    signs = sylvester(LANES).astype(jnp.bfloat16)
    product = sum(
        jnp.dot(part, signs, preferred_element_type=jnp.float32) for part in in_three(stacked)
    )
    return [product[at * rows : (at + 1) * rows] for at in range(len(tiles))]


def sketch_of(pseudo_grad, sign_flips, kept_rows):
    rows, block = pseudo_grad.shape
    keep = kept_rows.shape[1]
    count = block // LANES

    def kernel(grad_ref, signs_ref, kept_ref, out_ref):
        tiles = []
        for at in range(count):
            lanes = slice(at * LANES, (at + 1) * LANES)
            tiles.append(grad_ref[:, lanes] * signs_ref[:, lanes].astype(jnp.float32))
        spread = transform(tiles)
        for at in range(keep // LANES):
            lanes = slice(at * LANES, (at + 1) * LANES)
            kept = kept_ref[:, lanes]
            column = jnp.bitwise_and(kept, LANES - 1)
            tile = jnp.right_shift(kept, LANES.bit_length() - 1)
            picked = jnp.zeros((rows, LANES), jnp.float32)
            for other in range(count):
                values = jnp.take_along_axis(spread[other], column, axis=1)
                picked = jnp.where(tile == other, values, picked)
            out_ref[:, lanes] = picked * (block**-0.5)

    return pl.pallas_call(
        kernel,
        out_shape=jax.ShapeDtypeStruct((rows, keep), jnp.float32),
        in_specs=[pl.BlockSpec(memory_space=pltpu.VMEM)] * 3,
        out_specs=pl.BlockSpec(memory_space=pltpu.VMEM),
        compiler_params=pltpu.CompilerParams(vmem_limit_bytes=8 * MIB),
        cost_estimate=SMALL,
    )(pseudo_grad, sign_flips, kept_rows)


def outer_step(total, groups, kept_rows, sign_flips, momentum, fragment):
    rows, block = fragment.shape
    keep = kept_rows.shape[1]
    count = block // LANES
    scale = (block / keep) * block**-0.5

    def kernel(total_ref, kept_ref, signs_ref, momentum_ref, fragment_ref, *refs):
        fragment_out, momentum_out, placed = refs
        mean = total_ref[...] * (1.0 / groups)
        column = jnp.bitwise_and(kept_ref[...], LANES - 1)
        tile = jnp.right_shift(kept_ref[...], LANES.bit_length() - 1)
        tile_index = lax.broadcasted_iota(jnp.int32, (count, keep), 0)
        column_index = lax.broadcasted_iota(jnp.int32, (LANES, keep), 0)
        for row in range(rows):
            this = slice(row, row + 1)
            spots = jnp.where(tile[this] == tile_index, mean[this], 0.0)
            lines = jnp.where(column[this] == column_index, 1.0, 0.0).astype(jnp.bfloat16)
            sums = lax.dot_general(
                jnp.concatenate(in_three(spots), axis=0),
                lines,
                (((1,), (1,)), ((), ())),
                preferred_element_type=jnp.float32,
            )
            placed[row] = sums[:count] + sums[count : 2 * count] + sums[2 * count :]
        spread = transform([placed[:, at, :] for at in range(count)])
        for at in range(count):
            lanes = slice(at * LANES, (at + 1) * LANES)
            estimate = scale * signs_ref[:, lanes].astype(jnp.float32) * spread[at]
            momentum_now = 0.9 * momentum_ref[:, lanes] + estimate
            momentum_out[:, lanes] = momentum_now
            fragment_out[:, lanes] = fragment_ref[:, lanes] - 0.7 * (estimate + 0.9 * momentum_now)

    return pl.pallas_call(
        kernel,
        out_shape=[jax.ShapeDtypeStruct((rows, block), jnp.float32)] * 2,
        in_specs=[pl.BlockSpec(memory_space=pltpu.VMEM)] * 5,
        out_specs=[pl.BlockSpec(memory_space=pltpu.VMEM)] * 2,
        scratch_shapes=[pltpu.VMEM((rows, count, LANES), jnp.float32)],
        compiler_params=pltpu.CompilerParams(vmem_limit_bytes=8 * MIB),
        cost_estimate=SMALL,
    )(total, kept_rows, sign_flips, momentum, fragment)


def index_of(z, column, core):
    return z * 4 + column * 2 + core


def places():
    return [(z, y, c) for z in range(Z_WAYS) for y in range(2) for c in range(2)]


RING = [
    (index_of(z, y, c), index_of((z + 1 - 2 * c) % Z_WAYS, y, c)) for z, y, c in places()
]
COLUMN = [(index_of(z, y, c), index_of(z, 1 - y, c)) for z, y, c in places()]
CORE = [(index_of(z, y, c), index_of(z, y, 1 - c)) for z, y, c in places()]

FAR = (4, 3, 2, 1, 0)


class Place:
    def __init__(self):
        at = lax.axis_index("fsdp")
        self.z, self.column, self.core = at // 4, (at // 2) % 2, at % 2
        self.other, self.mate = 1 - self.column, 1 - self.core
        self.ahead = 1 - 2 * self.core

    def row(self, distance, other, mate):
        column = self.other if other is True else self.column
        if other in ("core", "mate"):
            column = (self.column + (self.core if other == "core" else self.mate)) % 2
        core = self.mate if mate else self.core
        return index_of((self.z + self.ahead * distance + 2 * Z_WAYS) % Z_WAYS, column, core)

    def runs(self, first):
        here, odd = self.z // 2, self.z % 2
        if first:
            return here, (here + 3 - 2 * odd) % 4
        return (here + 1 + 2 * odd) % 4, (here + 2) % 4


def ring(block):
    return lax.ppermute(block, "fsdp", RING)


def across(block):
    return lax.ppermute(block, "fsdp", COLUMN)


def twin(block):
    return lax.ppermute(block, "fsdp", CORE)


def replica_swap(total, distance):
    return lax.ppermute(total, "replica", [(at, at ^ distance) for at in range(2 * X_WAYS)])


def tie(values, deps):
    return list(lax.optimization_barrier((*values, *deps))[: len(values)])


def term_pieces(tokens, cotangent, scaling, parts, rows):
    (count, depth), width = tokens.shape, cotangent.shape[1]
    steps = depth // STEP
    counts = [len(blocks) for blocks in parts]
    ready = []
    for blocks in parts:
        before = max((4 + distance) % Z_WAYS for distance, _, _ in blocks)
        ready.append(min(-(-((before + 1) * 4 * rows + STEP - 1) // STEP), steps))

    def kernel(tokens_ref, cotangent_ref, *refs):
        place = Place()
        corner = ((place.z + 4) % Z_WAYS) * 4 * rows + place.core * (4 * rows - 1)
        walk = [
            ((corner // STEP + place.ahead * step + 2 * steps) % steps) * STEP
            for step in range(steps)
        ]
        starts = [place.row(*block) * rows for blocks in parts for block in blocks]
        outs, (term, held, other, sems, in_sems) = refs[: len(counts)], refs[len(counts) :]
        loads = [pltpu.make_async_copy(cotangent_ref, other, in_sems.at[steps])]
        for step in range(steps):
            lanes = pl.ds(pl.multiple_of(walk[step], STEP), STEP)
            loads.append(
                pltpu.make_async_copy(
                    tokens_ref.at[:, lanes], held.at[:, lanes], in_sems.at[step]
                )
            )
        for load in loads:
            load.start()
        copies = []
        for out, blocks in zip(outs, counts):
            for part in range(blocks):
                start = pl.multiple_of(starts[len(copies)], 16)
                copies.append(
                    pltpu.make_async_copy(
                        term.at[pl.ds(start, rows), :],
                        out.at[pl.ds(part * rows, rows), :],
                        sems.at[len(copies)],
                    )
                )
        loads[0].wait()
        for step in range(steps):
            loads[step + 1].wait()
            at = pl.multiple_of(walk[step], STEP)
            part = lax.dot_general(
                held[:, pl.ds(at, STEP)],
                other[...],
                (((0,), (0,)), ((), ())),
                preferred_element_type=jnp.float32,
            )
            term[pl.ds(at, STEP), :] = (part * scaling).astype(term.dtype)
            first = 0
            for blocks, after in zip(counts, ready):
                if after == step + 1:
                    for copy in copies[first : first + blocks]:
                        copy.start()
                first += blocks
        for copy in copies:
            copy.wait()

    return pl.pallas_call(
        kernel,
        out_shape=[jax.ShapeDtypeStruct((blocks * rows, width), jnp.bfloat16) for blocks in counts],
        in_specs=[pl.BlockSpec(memory_space=pl.ANY)] * 2,
        out_specs=[pl.BlockSpec(memory_space=pl.ANY)] * len(counts),
        scratch_shapes=[
            pltpu.VMEM((depth, width), jnp.bfloat16),
            pltpu.VMEM((count, depth), jnp.bfloat16),
            pltpu.VMEM((count, width), jnp.bfloat16),
            pltpu.SemaphoreType.DMA((sum(counts),)),
            pltpu.SemaphoreType.DMA((steps + 1,)),
        ],
        compiler_params=pltpu.CompilerParams(vmem_limit_bytes=LARGE),
        cost_estimate=pl.CostEstimate(
            flops=2 * count * depth * width, bytes_accessed=2 * depth * width, transcendentals=0
        ),
    )(tokens, cotangent)


def project(tokens, cotangent, pieces, rows, earlier=None):
    (count, depth), width = tokens.shape, cotangent.shape[1]
    run = depth // 4
    used = 2 * run // rows
    total = sum(len(blocks) for _, blocks in pieces)
    given = () if earlier is None else earlier

    def kernel(tokens_ref, cotangent_ref, *refs):
        place = Place()
        runs = place.runs(earlier is None)
        sources, refs = refs[: len(pieces)], refs[len(pieces) :]
        before, refs = refs[: len(given)], refs[len(given) :]
        token_grad, summed, weight, held, other, grads, part, keys, sems, in_sems, out_sems = refs
        loads = [pltpu.make_async_copy(cotangent_ref, other, in_sems.at[0])]
        spans = [pl.ds(pl.multiple_of(at_run * run, LANES), run) for at_run in runs]
        for at in range(2):
            loads.append(
                pltpu.make_async_copy(
                    tokens_ref.at[:, spans[at]],
                    held.at[:, at * run : (at + 1) * run],
                    in_sems.at[1 + at],
                )
            )
        if before:
            loads.append(pltpu.make_async_copy(before[1], part, in_sems.at[3]))
        for source, (_, blocks) in zip(sources, pieces):
            for at, block in enumerate(blocks):
                row = place.row(*block)
                slot = jnp.where(row // 8 == runs[0], row % 8, used + row % 4)
                slot = jnp.where(row // 8 == runs[1], used // 2 + row % 8, slot)
                start = pl.multiple_of(slot * rows, 16)
                pltpu.make_async_copy(
                    source.at[pl.ds(at * rows, rows), :],
                    weight.at[pl.ds(start, rows), :],
                    sems.at[slot],
                ).start()
        for load in loads:
            load.start()
        loads[0].wait()

        def wait_block(at):
            block = weight.at[pl.ds(at * rows, rows), :]
            pltpu.make_async_copy(block, block, sems.at[at]).wait()

        stores = []
        for at in range(2):
            mine = slice(at * run, (at + 1) * run)
            for block in range(at * used // 2, (at + 1) * used // 2):
                wait_block(block)
            grads[:, mine] = lax.dot_general(
                other[...],
                weight[mine, :],
                (((1,), (1,)), ((), ())),
                preferred_element_type=jnp.float32,
            ).astype(grads.dtype)
            stores.append(
                pltpu.make_async_copy(
                    grads.at[:, mine], token_grad.at[:, spans[at]], out_sems.at[at]
                )
            )
            stores[-1].start()
        for load in loads[1:]:
            load.wait()
        for at in range(0, width, STEP // 2):
            columns = slice(at, at + STEP // 2)
            product = jnp.dot(
                held[...], weight[: 2 * run, columns], preferred_element_type=jnp.float32
            )
            if before:
                keys[:, columns] = (part[:, columns] + product).astype(keys.dtype)
            else:
                part[:, columns] = product
        stores.append(pltpu.make_async_copy(keys if before else part, summed, out_sems.at[2]))
        stores[-1].start()
        for block in range(used, total):
            wait_block(block)
        for store in stores:
            store.wait()

    first_given = 2 + len(pieces)
    return pl.pallas_call(
        kernel,
        out_shape=[
            jax.ShapeDtypeStruct((count, depth), jnp.bfloat16),
            jax.ShapeDtypeStruct((count, width), jnp.bfloat16 if given else jnp.float32),
        ],
        in_specs=[pl.BlockSpec(memory_space=pl.ANY)] * (2 + len(pieces) + len(given)),
        out_specs=[pl.BlockSpec(memory_space=pl.ANY)] * 2,
        input_output_aliases={first_given: 0} if given else {},
        scratch_shapes=[
            pltpu.VMEM((total * rows, width), jnp.bfloat16),
            pltpu.VMEM((count, 2 * run), jnp.bfloat16),
            pltpu.VMEM((count, width), jnp.bfloat16),
            pltpu.VMEM((count, 2 * run), jnp.bfloat16),
            pltpu.VMEM((count, width), jnp.float32),
            pltpu.VMEM((count, width), jnp.bfloat16),
            pltpu.SemaphoreType.DMA((total,)),
            pltpu.SemaphoreType.DMA((4,)),
            pltpu.SemaphoreType.DMA((3,)),
        ],
        compiler_params=pltpu.CompilerParams(vmem_limit_bytes=LARGE),
        cost_estimate=SMALL,
    )(tokens, cotangent, *(block for block, _ in pieces), *given)


def join(first, second):
    rows, width = first.shape

    def kernel(first_ref, second_ref, out_ref, held, sems):
        halves = [held.at[pl.ds(0, rows), :], held.at[pl.ds(rows, rows), :]]
        loads = [
            pltpu.make_async_copy(source, half, sems.at[at])
            for at, (source, half) in enumerate(zip((first_ref, second_ref), halves))
        ]
        for load in loads:
            load.start()
        for load in loads:
            load.wait()
        store = pltpu.make_async_copy(held, out_ref, sems.at[2])
        store.start()
        store.wait()

    return pl.pallas_call(
        kernel,
        out_shape=jax.ShapeDtypeStruct((2 * rows, width), first.dtype),
        in_specs=[pl.BlockSpec(memory_space=pl.ANY)] * 2,
        out_specs=pl.BlockSpec(memory_space=pl.ANY),
        scratch_shapes=[
            pltpu.VMEM((2 * rows, width), first.dtype),
            pltpu.SemaphoreType.DMA((3,)),
        ],
        compiler_params=pltpu.CompilerParams(vmem_limit_bytes=8 * MIB),
        cost_estimate=SMALL,
    )(first, second)


def local(
    tokens, key_weight, key_cotangent, fragment, momentum, pseudo_grad, sign_flips, kept_rows
):
    own = key_weight[0]
    rows = own.shape[0]
    core = lax.axis_index("fsdp") % 2
    scaling = (tokens.shape[0] * lax.axis_size("fsdp")) ** (-0.5)
    wide, narrow = jnp.float32, jnp.bfloat16

    def then(block, before):
        return tie([block], [before])[0]

    own_twin, side = twin(own), across(own)
    first = [join(own, own_twin)]
    first.append(ring(first[0]))
    total = sketch_of(then(pseudo_grad[0], first[0]), sign_flips, kept_rows)
    swap = replica_swap(total, X_WAYS)

    def half(distance, other, rest=False):
        return [(distance, other, rest)]

    def pair(distance, other):
        return half(distance, other) + half(distance, other, True)

    kinds = [
        half(4, True) + pair(3, True),
        half(4, False) + pair(3, False),
        pair(2, True) + half(0, True),
        pair(2, False) + pair(1, False) + half(0, False),
        pair(1, True),
    ]
    parts = []
    for blocks in kinds:
        parts.append(blocks)
        parts.append([(-distance, other, not rest) for distance, other, rest in blocks])
    parts = term_pieces(then(tokens, total), key_cotangent, scaling, parts, rows)
    mine, theirs, got = list(parts[0::2]), list(parts[1::2]), [None] * 5

    def summed(part, at, extent):
        rows_there = slice(at, at + extent)
        return mine[part][rows_there].astype(wide) + got[part][rows_there].astype(wide)

    def onward(total, *others):
        for block in others:
            missing = total.shape[0] - block.shape[0]
            total = total + jnp.pad(block.astype(wide), ((0, missing), (0, 0)))
        total = total.astype(narrow)
        return total, ring(total)

    theirs[0], swap, side, first[1] = tie([theirs[0], swap, side, first[1]], [])
    total = total + swap
    got[0] = twin(theirs[0])
    side_twin = twin(side)
    first.append(ring(first[1]))
    first_twin = [None, twin(first[1])]
    got[0] = then(got[0], side_twin)
    step = summed(0, 0, 3 * rows).astype(narrow)
    over_43 = across(step)
    for part in range(1, 5):
        got[part] = twin(then(theirs[part], step))
    second = [join(*tie([side, side_twin], [step]))]
    second.append(ring(second[0]))
    got[2] = then(got[2], second[0])
    crossed = step = summed(2, 0, 3 * rows).astype(narrow)
    first[2] = step = then(first[2], step)
    first.append(ring(step))
    first_twin.append(twin(step))
    swap = replica_swap(then(total, step), 1)
    second[1], swap, step = tie([second[1], swap, step], [])
    total = total + swap
    second.append(ring(second[1]))
    second_twin = [None, twin(second[1])]
    first[3], step = tie([first[3], second[1]], [])
    first_twin.append(twin(first[3]))
    over_43, crossed = tie([over_43, crossed], [first[3], step])
    over_2 = across(crossed)
    step, come = onward(summed(1, 0, rows) + over_43[:rows].astype(wide))
    swap = replica_swap(then(total, step), 2)
    second[2], swap = tie([second[2], swap], [step])
    total = step = total + swap
    second.append(ring(second[2]))
    second_twin.append(twin(second[2]))
    come = then(come, step)
    step, come = onward(summed(1, rows, 2 * rows) + over_43[rows:].astype(wide), come)
    got[4] = then(got[4], step)
    crossed = summed(4, 0, 2 * rows).astype(narrow)
    new_fragment, new_momentum = outer_step(
        then(total, crossed), lax.axis_size("replica"), kept_rows, sign_flips, momentum, fragment
    )
    first_3, second[3] = tie([first[3], second[3]], [step, new_momentum])
    step = jnp.where(core == 0, first_3, second[3])
    last = ring(step)
    second_twin.append(twin(then(second[3], step)))
    over_2, come, crossed = tie([over_2, come, crossed], [step])
    over_1 = across(crossed)
    step, come = onward(summed(3, 0, 2 * rows) + over_2[: 2 * rows].astype(wide), come)

    def ring_pieces(distance):
        return [
            (first[distance], [(-distance, False, False), (-distance, False, True)]),
            (first_twin[distance], [(distance, False, True), (distance, False, False)]),
            (second[distance], [(-distance, True, False), (-distance, True, True)]),
            (second_twin[distance], [(distance, True, True), (distance, True, False)]),
        ]

    pieces = [
        (own, [(0, False, False)]),
        (own_twin, [(0, False, True)]),
        (side, [(0, True, False)]),
        (side_twin, [(0, True, True)]),
    ]
    earlier = project(
        then(tokens, step), key_cotangent, pieces + ring_pieces(1) + ring_pieces(2), rows
    )
    come = then(come, earlier[1])
    step, come = onward(summed(3, 2 * rows, 2 * rows) + over_1.astype(wide), come)
    last = then(last, step)
    last_twin = twin(last)
    step = last
    pieces = [
        (last, [(4, "core", False), (4, "core", True)]),
        (last_twin, [(4, "mate", True), (4, "mate", False)]),
    ]
    token_grad, projected = project(
        then(tokens, step), key_cotangent, ring_pieces(2) + ring_pieces(3) + pieces, rows, earlier
    )
    come = then(come, projected)
    rest = twin(come[rows:])
    weight_grad = (
        summed(3, 4 * rows, rows) + over_2[2 * rows :].astype(wide) + come[:rows].astype(wide) + rest.astype(wide)
    ).astype(narrow)[None]
    return (projected, token_grad, weight_grad, new_fragment, new_momentum)


def solution(mesh):
    placed = (
        P(("replica", "fsdp"), None),
        P("replica", "fsdp", None),
        P(("replica", "fsdp"), None),
        P("fsdp", None),
        P("fsdp", None),
        P("replica", "fsdp", None),
        P("fsdp", None),
        P("fsdp", None),
    )
    return jax.shard_map(
        local,
        mesh=mesh,
        in_specs=placed,
        out_specs=(
            P(("replica", "fsdp"), None),
            P(("replica", "fsdp"), None),
            P("replica", "fsdp", None),
            P("fsdp", None),
            P("fsdp", None),
        ),
        check_vma=False,
    )
```

```python
import jax
import jax.numpy as jnp
from jax import lax
from jax.experimental import pallas as pl
from jax.experimental.pallas import tpu as pltpu
from jax.sharding import PartitionSpec as P

LANES = 128
STEP = 512
MIB = 1024 * 1024
LARGE = 60 * MIB
SMALL = pl.CostEstimate(flops=1024, bytes_accessed=1024, transcendentals=0)
Z_WAYS = 8
X_WAYS = 4


def sylvester(extent):
    row_index = lax.broadcasted_iota(jnp.int32, (extent, extent), 0)
    col_index = lax.broadcasted_iota(jnp.int32, (extent, extent), 1)
    common = jnp.bitwise_and(row_index, col_index)
    parity = jnp.zeros((extent, extent), jnp.int32)
    for position in range(extent.bit_length()):
        parity = parity + jnp.bitwise_and(jnp.right_shift(common, position), 1)
    return (1 - 2 * jnp.bitwise_and(parity, 1)).astype(jnp.float32)


def in_three(values):
    high = values.astype(jnp.bfloat16)
    rest = values - high.astype(jnp.float32)
    middle = rest.astype(jnp.bfloat16)
    low = (rest - middle.astype(jnp.float32)).astype(jnp.bfloat16)
    return high, middle, low


def transform(tiles):
    tiles = list(tiles)
    distance = 1
    while distance < len(tiles):
        for at in range(len(tiles)):
            if at & distance == 0:
                low, high = tiles[at], tiles[at + distance]
                tiles[at], tiles[at + distance] = low + high, low - high
        distance *= 2
    rows = tiles[0].shape[0]
    stacked = jnp.concatenate(tiles, axis=0)
    signs = sylvester(LANES).astype(jnp.bfloat16)
    product = sum(
        jnp.dot(part, signs, preferred_element_type=jnp.float32) for part in in_three(stacked)
    )
    return [product[at * rows : (at + 1) * rows] for at in range(len(tiles))]


def sketch_of(pseudo_grad, sign_flips, kept_rows):
    rows, block = pseudo_grad.shape
    keep = kept_rows.shape[1]
    count = block // LANES

    def kernel(grad_ref, signs_ref, kept_ref, out_ref):
        tiles = []
        for at in range(count):
            lanes = slice(at * LANES, (at + 1) * LANES)
            tiles.append(grad_ref[:, lanes] * signs_ref[:, lanes].astype(jnp.float32))
        spread = transform(tiles)
        for at in range(keep // LANES):
            lanes = slice(at * LANES, (at + 1) * LANES)
            kept = kept_ref[:, lanes]
            column = jnp.bitwise_and(kept, LANES - 1)
            tile = jnp.right_shift(kept, LANES.bit_length() - 1)
            picked = jnp.zeros((rows, LANES), jnp.float32)
            for other in range(count):
                values = jnp.take_along_axis(spread[other], column, axis=1)
                picked = jnp.where(tile == other, values, picked)
            out_ref[:, lanes] = picked * (block**-0.5)

    return pl.pallas_call(
        kernel,
        out_shape=jax.ShapeDtypeStruct((rows, keep), jnp.float32),
        in_specs=[pl.BlockSpec(memory_space=pltpu.VMEM)] * 3,
        out_specs=pl.BlockSpec(memory_space=pltpu.VMEM),
        compiler_params=pltpu.CompilerParams(vmem_limit_bytes=8 * MIB),
        cost_estimate=SMALL,
    )(pseudo_grad, sign_flips, kept_rows)


def outer_step(total, groups, kept_rows, sign_flips, momentum, fragment):
    rows, block = fragment.shape
    keep = kept_rows.shape[1]
    count = block // LANES
    scale = (block / keep) * block**-0.5

    def kernel(total_ref, kept_ref, signs_ref, momentum_ref, fragment_ref, *refs):
        fragment_out, momentum_out, placed = refs
        mean = total_ref[...] * (1.0 / groups)
        column = jnp.bitwise_and(kept_ref[...], LANES - 1)
        tile = jnp.right_shift(kept_ref[...], LANES.bit_length() - 1)
        tile_index = lax.broadcasted_iota(jnp.int32, (count, keep), 0)
        column_index = lax.broadcasted_iota(jnp.int32, (LANES, keep), 0)
        for row in range(rows):
            this = slice(row, row + 1)
            spots = jnp.where(tile[this] == tile_index, mean[this], 0.0)
            lines = jnp.where(column[this] == column_index, 1.0, 0.0).astype(jnp.bfloat16)
            sums = lax.dot_general(
                jnp.concatenate(in_three(spots), axis=0),
                lines,
                (((1,), (1,)), ((), ())),
                preferred_element_type=jnp.float32,
            )
            placed[row] = sums[:count] + sums[count : 2 * count] + sums[2 * count :]
        spread = transform([placed[:, at, :] for at in range(count)])
        for at in range(count):
            lanes = slice(at * LANES, (at + 1) * LANES)
            estimate = scale * signs_ref[:, lanes].astype(jnp.float32) * spread[at]
            momentum_now = 0.9 * momentum_ref[:, lanes] + estimate
            momentum_out[:, lanes] = momentum_now
            fragment_out[:, lanes] = fragment_ref[:, lanes] - 0.7 * (estimate + 0.9 * momentum_now)

    return pl.pallas_call(
        kernel,
        out_shape=[jax.ShapeDtypeStruct((rows, block), jnp.float32)] * 2,
        in_specs=[pl.BlockSpec(memory_space=pltpu.VMEM)] * 5,
        out_specs=[pl.BlockSpec(memory_space=pltpu.VMEM)] * 2,
        scratch_shapes=[pltpu.VMEM((rows, count, LANES), jnp.float32)],
        compiler_params=pltpu.CompilerParams(vmem_limit_bytes=8 * MIB),
        cost_estimate=SMALL,
    )(total, kept_rows, sign_flips, momentum, fragment)


def index_of(z, column, core):
    return z * 4 + column * 2 + core


def places():
    return [(z, y, c) for z in range(Z_WAYS) for y in range(2) for c in range(2)]


RING = [
    (index_of(z, y, c), index_of((z + 1 - 2 * c) % Z_WAYS, y, c)) for z, y, c in places()
]
COLUMN = [(index_of(z, y, c), index_of(z, 1 - y, c)) for z, y, c in places()]
CORE = [(index_of(z, y, c), index_of(z, y, 1 - c)) for z, y, c in places()]

FAR = (4, 3, 2, 1, 0)


class Place:
    def __init__(self):
        at = lax.axis_index("fsdp")
        self.z, self.column, self.core = at // 4, (at // 2) % 2, at % 2
        self.other, self.mate = 1 - self.column, 1 - self.core
        self.ahead = 1 - 2 * self.core

    def row(self, distance, other, mate):
        column = self.other if other is True else self.column
        if other in ("core", "mate"):
            column = (self.column + (self.core if other == "core" else self.mate)) % 2
        core = self.mate if mate else self.core
        return index_of((self.z + self.ahead * distance + 2 * Z_WAYS) % Z_WAYS, column, core)

    def runs(self, first):
        here, odd = self.z // 2, self.z % 2
        if first:
            return here, (here + 3 - 2 * odd) % 4
        return (here + 1 + 2 * odd) % 4, (here + 2) % 4


def ring(block):
    return lax.ppermute(block, "fsdp", RING)


def across(block):
    return lax.ppermute(block, "fsdp", COLUMN)


def twin(block):
    return lax.ppermute(block, "fsdp", CORE)


def replica_swap(total, distance):
    return lax.ppermute(total, "replica", [(at, at ^ distance) for at in range(2 * X_WAYS)])


def tie(values, deps):
    return list(lax.optimization_barrier((*values, *deps))[: len(values)])


def term_pieces(tokens, cotangent, scaling, parts, rows):
    (count, depth), width = tokens.shape, cotangent.shape[1]
    steps = depth // STEP
    counts = [len(blocks) for blocks in parts]
    ready = []
    for blocks in parts:
        before = max((4 + distance) % Z_WAYS for distance, _, _ in blocks)
        ready.append(min(-(-((before + 1) * 4 * rows + STEP - 1) // STEP), steps))

    def kernel(tokens_ref, cotangent_ref, *refs):
        place = Place()
        corner = ((place.z + 4) % Z_WAYS) * 4 * rows + place.core * (4 * rows - 1)
        walk = [
            ((corner // STEP + place.ahead * step + 2 * steps) % steps) * STEP
            for step in range(steps)
        ]
        starts = [place.row(*block) * rows for blocks in parts for block in blocks]
        outs, (term, held, other, sems, in_sems) = refs[: len(counts)], refs[len(counts) :]
        loads = [pltpu.make_async_copy(cotangent_ref, other, in_sems.at[steps])]
        for step in range(steps):
            lanes = pl.ds(pl.multiple_of(walk[step], STEP), STEP)
            loads.append(
                pltpu.make_async_copy(
                    tokens_ref.at[:, lanes], held.at[:, lanes], in_sems.at[step]
                )
            )
        for load in loads:
            load.start()
        copies = []
        for out, blocks in zip(outs, counts):
            for part in range(blocks):
                start = pl.multiple_of(starts[len(copies)], 16)
                copies.append(
                    pltpu.make_async_copy(
                        term.at[pl.ds(start, rows), :],
                        out.at[pl.ds(part * rows, rows), :],
                        sems.at[len(copies)],
                    )
                )
        loads[0].wait()
        for step in range(steps):
            loads[step + 1].wait()
            at = pl.multiple_of(walk[step], STEP)
            part = lax.dot_general(
                held[:, pl.ds(at, STEP)],
                other[...],
                (((0,), (0,)), ((), ())),
                preferred_element_type=jnp.float32,
            )
            term[pl.ds(at, STEP), :] = (part * scaling).astype(term.dtype)
            first = 0
            for blocks, after in zip(counts, ready):
                if after == step + 1:
                    for copy in copies[first : first + blocks]:
                        copy.start()
                first += blocks
        for copy in copies:
            copy.wait()

    return pl.pallas_call(
        kernel,
        out_shape=[jax.ShapeDtypeStruct((blocks * rows, width), jnp.bfloat16) for blocks in counts],
        in_specs=[pl.BlockSpec(memory_space=pl.ANY)] * 2,
        out_specs=[pl.BlockSpec(memory_space=pl.ANY)] * len(counts),
        scratch_shapes=[
            pltpu.VMEM((depth, width), jnp.bfloat16),
            pltpu.VMEM((count, depth), jnp.bfloat16),
            pltpu.VMEM((count, width), jnp.bfloat16),
            pltpu.SemaphoreType.DMA((sum(counts),)),
            pltpu.SemaphoreType.DMA((steps + 1,)),
        ],
        compiler_params=pltpu.CompilerParams(vmem_limit_bytes=LARGE),
        cost_estimate=pl.CostEstimate(
            flops=2 * count * depth * width, bytes_accessed=2 * depth * width, transcendentals=0
        ),
    )(tokens, cotangent)


def project(tokens, cotangent, pieces, rows, earlier=None):
    (count, depth), width = tokens.shape, cotangent.shape[1]
    run = depth // 4
    used = 2 * run // rows
    total = sum(len(blocks) for _, blocks in pieces)
    given = () if earlier is None else earlier

    def kernel(tokens_ref, cotangent_ref, *refs):
        place = Place()
        runs = place.runs(earlier is None)
        sources, refs = refs[: len(pieces)], refs[len(pieces) :]
        before, refs = refs[: len(given)], refs[len(given) :]
        token_grad, summed, weight, held, other, grads, part, keys, sems, in_sems, out_sems = refs
        loads = [pltpu.make_async_copy(cotangent_ref, other, in_sems.at[0])]
        spans = [pl.ds(pl.multiple_of(at_run * run, LANES), run) for at_run in runs]
        for at in range(2):
            loads.append(
                pltpu.make_async_copy(
                    tokens_ref.at[:, spans[at]],
                    held.at[:, at * run : (at + 1) * run],
                    in_sems.at[1 + at],
                )
            )
        if before:
            loads.append(pltpu.make_async_copy(before[1], part, in_sems.at[3]))
        for source, (_, blocks) in zip(sources, pieces):
            for at, block in enumerate(blocks):
                row = place.row(*block)
                slot = jnp.where(row // 8 == runs[0], row % 8, used + row % 4)
                slot = jnp.where(row // 8 == runs[1], used // 2 + row % 8, slot)
                start = pl.multiple_of(slot * rows, 16)
                pltpu.make_async_copy(
                    source.at[pl.ds(at * rows, rows), :],
                    weight.at[pl.ds(start, rows), :],
                    sems.at[slot],
                ).start()
        for load in loads:
            load.start()
        loads[0].wait()

        def wait_block(at):
            block = weight.at[pl.ds(at * rows, rows), :]
            pltpu.make_async_copy(block, block, sems.at[at]).wait()

        stores = []
        for at in range(2):
            mine = slice(at * run, (at + 1) * run)
            for block in range(at * used // 2, (at + 1) * used // 2):
                wait_block(block)
            grads[:, mine] = lax.dot_general(
                other[...],
                weight[mine, :],
                (((1,), (1,)), ((), ())),
                preferred_element_type=jnp.float32,
            ).astype(grads.dtype)
            stores.append(
                pltpu.make_async_copy(
                    grads.at[:, mine], token_grad.at[:, spans[at]], out_sems.at[at]
                )
            )
            stores[-1].start()
        for load in loads[1:]:
            load.wait()
        for at in range(0, width, STEP // 2):
            columns = slice(at, at + STEP // 2)
            product = jnp.dot(
                held[...], weight[: 2 * run, columns], preferred_element_type=jnp.float32
            )
            if before:
                keys[:, columns] = (part[:, columns] + product).astype(keys.dtype)
            else:
                part[:, columns] = product
        stores.append(pltpu.make_async_copy(keys if before else part, summed, out_sems.at[2]))
        stores[-1].start()
        for block in range(used, total):
            wait_block(block)
        for store in stores:
            store.wait()

    first_given = 2 + len(pieces)
    return pl.pallas_call(
        kernel,
        out_shape=[
            jax.ShapeDtypeStruct((count, depth), jnp.bfloat16),
            jax.ShapeDtypeStruct((count, width), jnp.bfloat16 if given else jnp.float32),
        ],
        in_specs=[pl.BlockSpec(memory_space=pl.ANY)] * (2 + len(pieces) + len(given)),
        out_specs=[pl.BlockSpec(memory_space=pl.ANY)] * 2,
        input_output_aliases={first_given: 0} if given else {},
        scratch_shapes=[
            pltpu.VMEM((total * rows, width), jnp.bfloat16),
            pltpu.VMEM((count, 2 * run), jnp.bfloat16),
            pltpu.VMEM((count, width), jnp.bfloat16),
            pltpu.VMEM((count, 2 * run), jnp.bfloat16),
            pltpu.VMEM((count, width), jnp.float32),
            pltpu.VMEM((count, width), jnp.bfloat16),
            pltpu.SemaphoreType.DMA((total,)),
            pltpu.SemaphoreType.DMA((4,)),
            pltpu.SemaphoreType.DMA((3,)),
        ],
        compiler_params=pltpu.CompilerParams(vmem_limit_bytes=LARGE),
        cost_estimate=SMALL,
    )(tokens, cotangent, *(block for block, _ in pieces), *given)


def join(first, second):
    rows, width = first.shape

    def kernel(first_ref, second_ref, out_ref, held, sems):
        halves = [held.at[pl.ds(0, rows), :], held.at[pl.ds(rows, rows), :]]
        loads = [
            pltpu.make_async_copy(source, half, sems.at[at])
            for at, (source, half) in enumerate(zip((first_ref, second_ref), halves))
        ]
        for load in loads:
            load.start()
        for load in loads:
            load.wait()
        store = pltpu.make_async_copy(held, out_ref, sems.at[2])
        store.start()
        store.wait()

    return pl.pallas_call(
        kernel,
        out_shape=jax.ShapeDtypeStruct((2 * rows, width), first.dtype),
        in_specs=[pl.BlockSpec(memory_space=pl.ANY)] * 2,
        out_specs=pl.BlockSpec(memory_space=pl.ANY),
        scratch_shapes=[
            pltpu.VMEM((2 * rows, width), first.dtype),
            pltpu.SemaphoreType.DMA((3,)),
        ],
        compiler_params=pltpu.CompilerParams(vmem_limit_bytes=8 * MIB),
        cost_estimate=SMALL,
    )(first, second)


def local(
    tokens, key_weight, key_cotangent, fragment, momentum, pseudo_grad, sign_flips, kept_rows
):
    own = key_weight[0]
    rows = own.shape[0]
    core = lax.axis_index("fsdp") % 2
    scaling = (tokens.shape[0] * lax.axis_size("fsdp")) ** (-0.5)
    wide, narrow = jnp.float32, jnp.bfloat16

    def then(block, before):
        return tie([block], [before])[0]

    own_twin, side = twin(own), across(own)
    first = [join(own, own_twin)]
    first.append(ring(first[0]))
    def half(distance, other, rest=False):
        return [(distance, other, rest)]

    def pair(distance, other):
        return half(distance, other) + half(distance, other, True)

    kinds = [
        half(4, True) + pair(3, True),
        half(4, False) + pair(3, False),
        pair(2, True) + half(0, True),
        pair(2, False) + pair(1, False) + half(0, False),
        pair(1, True),
    ]
    parts = []
    for blocks in kinds:
        parts.append(blocks)
        parts.append([(-distance, other, not rest) for distance, other, rest in blocks])
    parts = term_pieces(then(tokens, first[0]), key_cotangent, scaling, parts, rows)
    mine, theirs, got = list(parts[0::2]), list(parts[1::2]), [None] * 5

    def summed(part, at, extent):
        rows_there = slice(at, at + extent)
        return mine[part][rows_there].astype(wide) + got[part][rows_there].astype(wide)

    def onward(total, *others):
        for block in others:
            missing = total.shape[0] - block.shape[0]
            total = total + jnp.pad(block.astype(wide), ((0, missing), (0, 0)))
        total = total.astype(narrow)
        return total, ring(total)

    theirs[0], side, first[1] = tie([theirs[0], side, first[1]], [])
    got[0] = twin(theirs[0])
    total = sketch_of(then(pseudo_grad[0], theirs[0]), sign_flips, kept_rows)
    side_twin = twin(side)
    first.append(ring(first[1]))
    first_twin = [None, twin(first[1])]
    got[0], side_twin = tie([got[0], side_twin], [total])
    step = summed(0, 0, 3 * rows).astype(narrow)
    over_43 = across(step)
    for part in range(1, 5):
        got[part] = twin(then(theirs[part], step))
    second = [join(*tie([side, side_twin], [step]))]
    second.append(ring(second[0]))
    got[2] = then(got[2], second[0])
    crossed = step = summed(2, 0, 3 * rows).astype(narrow)
    first[2] = step = then(first[2], step)
    first.append(ring(step))
    first_twin.append(twin(step))
    swap = replica_swap(then(total, step), 1)
    second[1], swap, step = tie([second[1], swap, step], [])
    total = total + swap
    swap = replica_swap(total, 2)
    second.append(ring(second[1]))
    second_twin = [None, twin(second[1])]
    first[3], step, swap = tie([first[3], second[1], swap], [])
    total = total + swap
    first_twin.append(twin(first[3]))
    over_43, crossed = tie([over_43, crossed], [first[3], step])
    over_2 = across(crossed)
    step, come = onward(summed(1, 0, rows) + over_43[:rows].astype(wide))
    second[2] = step = then(second[2], step)
    swap = replica_swap(then(total, step), X_WAYS)
    second.append(ring(second[2]))
    second_twin.append(twin(second[2]))
    come = then(come, step)
    step, come = onward(summed(1, rows, 2 * rows) + over_43[rows:].astype(wide), come)
    got[4] = then(got[4], step)
    crossed = summed(4, 0, 2 * rows).astype(narrow)
    first_3, second[3] = tie([first[3], second[3]], [step, crossed])
    step = jnp.where(core == 0, first_3, second[3])
    last = ring(step)
    second_twin.append(twin(then(second[3], step)))
    total = total + then(swap, step)
    over_2, come, crossed = tie([over_2, come, crossed], [total])
    over_1 = across(crossed)
    step, come = onward(summed(3, 0, 2 * rows) + over_2[: 2 * rows].astype(wide), come)

    def ring_pieces(distance):
        return [
            (first[distance], [(-distance, False, False), (-distance, False, True)]),
            (first_twin[distance], [(distance, False, True), (distance, False, False)]),
            (second[distance], [(-distance, True, False), (-distance, True, True)]),
            (second_twin[distance], [(distance, True, True), (distance, True, False)]),
        ]

    pieces = [
        (own, [(0, False, False)]),
        (own_twin, [(0, False, True)]),
        (side, [(0, True, False)]),
        (side_twin, [(0, True, True)]),
    ]
    earlier = project(
        then(tokens, step), key_cotangent, pieces + ring_pieces(1) + ring_pieces(2), rows
    )
    new_fragment, new_momentum = outer_step(
        then(total, earlier[1]),
        lax.axis_size("replica"),
        kept_rows,
        sign_flips,
        momentum,
        fragment,
    )
    come = then(come, new_momentum)
    step, come = onward(summed(3, 2 * rows, 2 * rows) + over_1.astype(wide), come)
    last = then(last, step)
    last_twin = twin(last)
    step = last
    pieces = [
        (last, [(4, "core", False), (4, "core", True)]),
        (last_twin, [(4, "mate", True), (4, "mate", False)]),
    ]
    token_grad, projected = project(
        then(tokens, step), key_cotangent, ring_pieces(2) + ring_pieces(3) + pieces, rows, earlier
    )
    come = then(come, projected)
    rest = twin(come[rows:])
    weight_grad = (
        summed(3, 4 * rows, rows) + over_2[2 * rows :].astype(wide) + come[:rows].astype(wide) + rest.astype(wide)
    ).astype(narrow)[None]
    return (projected, token_grad, weight_grad, new_fragment, new_momentum)


def solution(mesh):
    placed = (
        P(("replica", "fsdp"), None),
        P("replica", "fsdp", None),
        P(("replica", "fsdp"), None),
        P("fsdp", None),
        P("fsdp", None),
        P("replica", "fsdp", None),
        P("fsdp", None),
        P("fsdp", None),
    )
    return jax.shard_map(
        local,
        mesh=mesh,
        in_specs=placed,
        out_specs=(
            P(("replica", "fsdp"), None),
            P(("replica", "fsdp"), None),
            P("replica", "fsdp", None),
            P("fsdp", None),
            P("fsdp", None),
        ),
        check_vma=False,
    )
```

```python
import jax
import jax.numpy as jnp
from jax import lax
from jax.experimental import pallas as pl
from jax.experimental.pallas import tpu as pltpu
from jax.sharding import PartitionSpec as P

LANES = 128
STEP = 512
MIB = 1024 * 1024
LARGE = 60 * MIB
SMALL = pl.CostEstimate(flops=1024, bytes_accessed=1024, transcendentals=0)
Z_WAYS = 8
X_WAYS = 4


def sylvester(extent):
    row_index = lax.broadcasted_iota(jnp.int32, (extent, extent), 0)
    col_index = lax.broadcasted_iota(jnp.int32, (extent, extent), 1)
    common = jnp.bitwise_and(row_index, col_index)
    parity = jnp.zeros((extent, extent), jnp.int32)
    for position in range(extent.bit_length()):
        parity = parity + jnp.bitwise_and(jnp.right_shift(common, position), 1)
    return (1 - 2 * jnp.bitwise_and(parity, 1)).astype(jnp.float32)


def in_three(values):
    high = values.astype(jnp.bfloat16)
    rest = values - high.astype(jnp.float32)
    middle = rest.astype(jnp.bfloat16)
    low = (rest - middle.astype(jnp.float32)).astype(jnp.bfloat16)
    return high, middle, low


def transform(tiles):
    tiles = list(tiles)
    distance = 1
    while distance < len(tiles):
        for at in range(len(tiles)):
            if at & distance == 0:
                low, high = tiles[at], tiles[at + distance]
                tiles[at], tiles[at + distance] = low + high, low - high
        distance *= 2
    rows = tiles[0].shape[0]
    stacked = jnp.concatenate(tiles, axis=0)
    signs = sylvester(LANES).astype(jnp.bfloat16)
    product = sum(
        jnp.dot(part, signs, preferred_element_type=jnp.float32) for part in in_three(stacked)
    )
    return [product[at * rows : (at + 1) * rows] for at in range(len(tiles))]


def sketch_of(pseudo_grad, sign_flips, kept_rows):
    rows, block = pseudo_grad.shape
    keep = kept_rows.shape[1]
    count = block // LANES

    def kernel(grad_ref, signs_ref, kept_ref, out_ref):
        tiles = []
        for at in range(count):
            lanes = slice(at * LANES, (at + 1) * LANES)
            tiles.append(grad_ref[:, lanes] * signs_ref[:, lanes].astype(jnp.float32))
        spread = transform(tiles)
        for at in range(keep // LANES):
            lanes = slice(at * LANES, (at + 1) * LANES)
            kept = kept_ref[:, lanes]
            column = jnp.bitwise_and(kept, LANES - 1)
            tile = jnp.right_shift(kept, LANES.bit_length() - 1)
            picked = jnp.zeros((rows, LANES), jnp.float32)
            for other in range(count):
                values = jnp.take_along_axis(spread[other], column, axis=1)
                picked = jnp.where(tile == other, values, picked)
            out_ref[:, lanes] = picked * (block**-0.5)

    return pl.pallas_call(
        kernel,
        out_shape=jax.ShapeDtypeStruct((rows, keep), jnp.float32),
        in_specs=[pl.BlockSpec(memory_space=pltpu.VMEM)] * 3,
        out_specs=pl.BlockSpec(memory_space=pltpu.VMEM),
        compiler_params=pltpu.CompilerParams(vmem_limit_bytes=8 * MIB),
        cost_estimate=SMALL,
    )(pseudo_grad, sign_flips, kept_rows)


def outer_step(total, groups, kept_rows, sign_flips, momentum, fragment):
    rows, block = fragment.shape
    keep = kept_rows.shape[1]
    count = block // LANES
    scale = (block / keep) * block**-0.5

    def kernel(total_ref, kept_ref, signs_ref, momentum_ref, fragment_ref, *refs):
        fragment_out, momentum_out, placed = refs
        mean = total_ref[...] * (1.0 / groups)
        column = jnp.bitwise_and(kept_ref[...], LANES - 1)
        tile = jnp.right_shift(kept_ref[...], LANES.bit_length() - 1)
        tile_index = lax.broadcasted_iota(jnp.int32, (count, keep), 0)
        column_index = lax.broadcasted_iota(jnp.int32, (LANES, keep), 0)
        for row in range(rows):
            this = slice(row, row + 1)
            spots = jnp.where(tile[this] == tile_index, mean[this], 0.0)
            lines = jnp.where(column[this] == column_index, 1.0, 0.0).astype(jnp.bfloat16)
            sums = lax.dot_general(
                jnp.concatenate(in_three(spots), axis=0),
                lines,
                (((1,), (1,)), ((), ())),
                preferred_element_type=jnp.float32,
            )
            placed[row] = sums[:count] + sums[count : 2 * count] + sums[2 * count :]
        spread = transform([placed[:, at, :] for at in range(count)])
        for at in range(count):
            lanes = slice(at * LANES, (at + 1) * LANES)
            estimate = scale * signs_ref[:, lanes].astype(jnp.float32) * spread[at]
            momentum_now = 0.9 * momentum_ref[:, lanes] + estimate
            momentum_out[:, lanes] = momentum_now
            fragment_out[:, lanes] = fragment_ref[:, lanes] - 0.7 * (estimate + 0.9 * momentum_now)

    return pl.pallas_call(
        kernel,
        out_shape=[jax.ShapeDtypeStruct((rows, block), jnp.float32)] * 2,
        in_specs=[pl.BlockSpec(memory_space=pltpu.VMEM)] * 5,
        out_specs=[pl.BlockSpec(memory_space=pltpu.VMEM)] * 2,
        scratch_shapes=[pltpu.VMEM((rows, count, LANES), jnp.float32)],
        compiler_params=pltpu.CompilerParams(vmem_limit_bytes=8 * MIB),
        cost_estimate=SMALL,
    )(total, kept_rows, sign_flips, momentum, fragment)


def index_of(z, column, core):
    return z * 4 + column * 2 + core


def places():
    return [(z, y, c) for z in range(Z_WAYS) for y in range(2) for c in range(2)]


RING = [
    (index_of(z, y, c), index_of((z + 1 - 2 * c) % Z_WAYS, y, c)) for z, y, c in places()
]
COLUMN = [(index_of(z, y, c), index_of(z, 1 - y, c)) for z, y, c in places()]
CORE = [(index_of(z, y, c), index_of(z, y, 1 - c)) for z, y, c in places()]

FAR = (4, 3, 2, 1, 0)


class Place:
    def __init__(self):
        at = lax.axis_index("fsdp")
        self.z, self.column, self.core = at // 4, (at // 2) % 2, at % 2
        self.other, self.mate = 1 - self.column, 1 - self.core
        self.ahead = 1 - 2 * self.core

    def row(self, distance, other, mate):
        column = self.other if other is True else self.column
        if other in ("core", "mate"):
            column = (self.column + (self.core if other == "core" else self.mate)) % 2
        core = self.mate if mate else self.core
        return index_of((self.z + self.ahead * distance + 2 * Z_WAYS) % Z_WAYS, column, core)

    def runs(self, first):
        here, odd = self.z // 2, self.z % 2
        if first:
            return here, (here + 3 - 2 * odd) % 4
        return (here + 1 + 2 * odd) % 4, (here + 2) % 4


def ring(block):
    return lax.ppermute(block, "fsdp", RING)


def across(block):
    return lax.ppermute(block, "fsdp", COLUMN)


def twin(block):
    return lax.ppermute(block, "fsdp", CORE)


def replica_swap(total, distance):
    return lax.ppermute(total, "replica", [(at, at ^ distance) for at in range(2 * X_WAYS)])


def tie(values, deps):
    return list(lax.optimization_barrier((*values, *deps))[: len(values)])


def term_pieces(tokens, cotangent, scaling, parts, rows):
    (count, depth), width = tokens.shape, cotangent.shape[1]
    steps = depth // STEP
    counts = [len(blocks) for blocks in parts]
    ready = []
    for blocks in parts:
        before = max((4 + distance) % Z_WAYS for distance, _, _ in blocks)
        ready.append(min(-(-((before + 1) * 4 * rows + STEP - 1) // STEP), steps))

    def kernel(tokens_ref, cotangent_ref, *refs):
        place = Place()
        corner = ((place.z + 4) % Z_WAYS) * 4 * rows + place.core * (4 * rows - 1)
        walk = [
            ((corner // STEP + place.ahead * step + 2 * steps) % steps) * STEP
            for step in range(steps)
        ]
        starts = [place.row(*block) * rows for blocks in parts for block in blocks]
        outs, (term, held, other, sems, in_sems) = refs[: len(counts)], refs[len(counts) :]
        loads = [pltpu.make_async_copy(cotangent_ref, other, in_sems.at[steps])]
        for step in range(steps):
            lanes = pl.ds(pl.multiple_of(walk[step], STEP), STEP)
            loads.append(
                pltpu.make_async_copy(
                    tokens_ref.at[:, lanes], held.at[:, lanes], in_sems.at[step]
                )
            )
        for load in loads:
            load.start()
        copies = []
        for out, blocks in zip(outs, counts):
            for part in range(blocks):
                start = pl.multiple_of(starts[len(copies)], 16)
                copies.append(
                    pltpu.make_async_copy(
                        term.at[pl.ds(start, rows), :],
                        out.at[pl.ds(part * rows, rows), :],
                        sems.at[len(copies)],
                    )
                )
        loads[0].wait()
        for step in range(steps):
            loads[step + 1].wait()
            at = pl.multiple_of(walk[step], STEP)
            part = lax.dot_general(
                held[:, pl.ds(at, STEP)],
                other[...],
                (((0,), (0,)), ((), ())),
                preferred_element_type=jnp.float32,
            )
            term[pl.ds(at, STEP), :] = (part * scaling).astype(term.dtype)
            first = 0
            for blocks, after in zip(counts, ready):
                if after == step + 1:
                    for copy in copies[first : first + blocks]:
                        copy.start()
                first += blocks
        for copy in copies:
            copy.wait()

    return pl.pallas_call(
        kernel,
        out_shape=[jax.ShapeDtypeStruct((blocks * rows, width), jnp.bfloat16) for blocks in counts],
        in_specs=[pl.BlockSpec(memory_space=pl.ANY)] * 2,
        out_specs=[pl.BlockSpec(memory_space=pl.ANY)] * len(counts),
        scratch_shapes=[
            pltpu.VMEM((depth, width), jnp.bfloat16),
            pltpu.VMEM((count, depth), jnp.bfloat16),
            pltpu.VMEM((count, width), jnp.bfloat16),
            pltpu.SemaphoreType.DMA((sum(counts),)),
            pltpu.SemaphoreType.DMA((steps + 1,)),
        ],
        compiler_params=pltpu.CompilerParams(vmem_limit_bytes=LARGE),
        cost_estimate=pl.CostEstimate(
            flops=2 * count * depth * width, bytes_accessed=2 * depth * width, transcendentals=0
        ),
    )(tokens, cotangent)


def project(tokens, cotangent, pieces, rows, earlier=None):
    (count, depth), width = tokens.shape, cotangent.shape[1]
    run = depth // 4
    used = 2 * run // rows
    total = sum(len(blocks) for _, blocks in pieces)
    given = () if earlier is None else earlier

    def kernel(tokens_ref, cotangent_ref, *refs):
        place = Place()
        runs = place.runs(earlier is None)
        sources, refs = refs[: len(pieces)], refs[len(pieces) :]
        before, refs = refs[: len(given)], refs[len(given) :]
        token_grad, summed, weight, held, other, grads, part, keys, sems, in_sems, out_sems = refs
        loads = [pltpu.make_async_copy(cotangent_ref, other, in_sems.at[0])]
        spans = [pl.ds(pl.multiple_of(at_run * run, LANES), run) for at_run in runs]
        for at in range(2):
            loads.append(
                pltpu.make_async_copy(
                    tokens_ref.at[:, spans[at]],
                    held.at[:, at * run : (at + 1) * run],
                    in_sems.at[1 + at],
                )
            )
        if before:
            loads.append(pltpu.make_async_copy(before[1], part, in_sems.at[3]))
        for source, (_, blocks) in zip(sources, pieces):
            for at, block in enumerate(blocks):
                row = place.row(*block)
                slot = jnp.where(row // 8 == runs[0], row % 8, used + row % 4)
                slot = jnp.where(row // 8 == runs[1], used // 2 + row % 8, slot)
                start = pl.multiple_of(slot * rows, 16)
                pltpu.make_async_copy(
                    source.at[pl.ds(at * rows, rows), :],
                    weight.at[pl.ds(start, rows), :],
                    sems.at[slot],
                ).start()
        for load in loads:
            load.start()
        loads[0].wait()

        def wait_block(at):
            block = weight.at[pl.ds(at * rows, rows), :]
            pltpu.make_async_copy(block, block, sems.at[at]).wait()

        stores = []
        for at in range(2):
            mine = slice(at * run, (at + 1) * run)
            for block in range(at * used // 2, (at + 1) * used // 2):
                wait_block(block)
            grads[:, mine] = lax.dot_general(
                other[...],
                weight[mine, :],
                (((1,), (1,)), ((), ())),
                preferred_element_type=jnp.float32,
            ).astype(grads.dtype)
            stores.append(
                pltpu.make_async_copy(
                    grads.at[:, mine], token_grad.at[:, spans[at]], out_sems.at[at]
                )
            )
            stores[-1].start()
        for load in loads[1:]:
            load.wait()
        for at in range(0, width, STEP // 2):
            columns = slice(at, at + STEP // 2)
            product = jnp.dot(
                held[...], weight[: 2 * run, columns], preferred_element_type=jnp.float32
            )
            if before:
                keys[:, columns] = (part[:, columns] + product).astype(keys.dtype)
            else:
                part[:, columns] = product
        stores.append(pltpu.make_async_copy(keys if before else part, summed, out_sems.at[2]))
        stores[-1].start()
        for block in range(used, total):
            wait_block(block)
        for store in stores:
            store.wait()

    first_given = 2 + len(pieces)
    return pl.pallas_call(
        kernel,
        out_shape=[
            jax.ShapeDtypeStruct((count, depth), jnp.bfloat16),
            jax.ShapeDtypeStruct((count, width), jnp.bfloat16 if given else jnp.float32),
        ],
        in_specs=[pl.BlockSpec(memory_space=pl.ANY)] * (2 + len(pieces) + len(given)),
        out_specs=[pl.BlockSpec(memory_space=pl.ANY)] * 2,
        input_output_aliases={first_given: 0} if given else {},
        scratch_shapes=[
            pltpu.VMEM((total * rows, width), jnp.bfloat16),
            pltpu.VMEM((count, 2 * run), jnp.bfloat16),
            pltpu.VMEM((count, width), jnp.bfloat16),
            pltpu.VMEM((count, 2 * run), jnp.bfloat16),
            pltpu.VMEM((count, width), jnp.float32),
            pltpu.VMEM((count, width), jnp.bfloat16),
            pltpu.SemaphoreType.DMA((total,)),
            pltpu.SemaphoreType.DMA((4,)),
            pltpu.SemaphoreType.DMA((3,)),
        ],
        compiler_params=pltpu.CompilerParams(vmem_limit_bytes=LARGE),
        cost_estimate=SMALL,
    )(tokens, cotangent, *(block for block, _ in pieces), *given)


def join(first, second):
    rows, width = first.shape

    def kernel(first_ref, second_ref, out_ref, held, sems):
        halves = [held.at[pl.ds(0, rows), :], held.at[pl.ds(rows, rows), :]]
        loads = [
            pltpu.make_async_copy(source, half, sems.at[at])
            for at, (source, half) in enumerate(zip((first_ref, second_ref), halves))
        ]
        for load in loads:
            load.start()
        for load in loads:
            load.wait()
        store = pltpu.make_async_copy(held, out_ref, sems.at[2])
        store.start()
        store.wait()

    return pl.pallas_call(
        kernel,
        out_shape=jax.ShapeDtypeStruct((2 * rows, width), first.dtype),
        in_specs=[pl.BlockSpec(memory_space=pl.ANY)] * 2,
        out_specs=pl.BlockSpec(memory_space=pl.ANY),
        scratch_shapes=[
            pltpu.VMEM((2 * rows, width), first.dtype),
            pltpu.SemaphoreType.DMA((3,)),
        ],
        compiler_params=pltpu.CompilerParams(vmem_limit_bytes=8 * MIB),
        cost_estimate=SMALL,
    )(first, second)


def local(
    tokens, key_weight, key_cotangent, fragment, momentum, pseudo_grad, sign_flips, kept_rows
):
    own = key_weight[0]
    rows = own.shape[0]
    core = lax.axis_index("fsdp") % 2
    scaling = (tokens.shape[0] * lax.axis_size("fsdp")) ** (-0.5)
    wide, narrow = jnp.float32, jnp.bfloat16

    def then(block, before):
        return tie([block], [before])[0]

    own_twin, side = twin(own), across(own)
    first = [join(own, own_twin)]
    first.append(ring(first[0]))
    def half(distance, other, rest=False):
        return [(distance, other, rest)]

    def pair(distance, other):
        return half(distance, other) + half(distance, other, True)

    kinds = [
        half(4, True) + pair(3, True),
        half(4, False) + pair(3, False),
        pair(2, True) + half(0, True),
        pair(2, False),
        pair(1, True),
        pair(1, False) + half(0, False),
    ]
    parts = []
    for blocks in kinds:
        parts.append(blocks)
        parts.append([(-distance, other, not rest) for distance, other, rest in blocks])
    parts = term_pieces(then(tokens, first[0]), key_cotangent, scaling, parts, rows)
    mine, theirs, got = list(parts[0::2]), list(parts[1::2]), [None] * 6

    def summed(part, at, extent):
        rows_there = slice(at, at + extent)
        return mine[part][rows_there].astype(wide) + got[part][rows_there].astype(wide)

    def onward(total, *others):
        for block in others:
            missing = total.shape[0] - block.shape[0]
            total = total + jnp.pad(block.astype(wide), ((0, missing), (0, 0)))
        total = total.astype(narrow)
        return total, ring(total)

    theirs[0], side, first[1] = tie([theirs[0], side, first[1]], [])
    got[0] = twin(theirs[0])
    total = sketch_of(then(pseudo_grad[0], theirs[0]), sign_flips, kept_rows)
    side_twin = twin(side)
    first.append(ring(first[1]))
    first_twin = [None, twin(first[1])]
    got[0], side_twin = tie([got[0], side_twin], [total])
    step = summed(0, 0, 3 * rows).astype(narrow)
    over_43 = across(step)
    for part in range(1, 6):
        got[part] = twin(then(theirs[part], step))
    second = [join(*tie([side, side_twin], [step]))]
    second.append(ring(second[0]))
    got[2] = then(got[2], second[0])
    crossed = step = summed(2, 0, 3 * rows).astype(narrow)
    first[2] = step = then(first[2], step)
    first.append(ring(step))
    first_twin.append(twin(step))
    swap = replica_swap(then(total, step), 1)
    second[1], swap, step = tie([second[1], swap, step], [])
    total = total + swap
    swap = replica_swap(total, 2)
    second.append(ring(second[1]))
    second_twin = [None, twin(second[1])]
    first[3], step, swap = tie([first[3], second[1], swap], [])
    total = total + swap
    first_twin.append(twin(first[3]))
    over_43, crossed = tie([over_43, crossed], [first[3], step])
    over_2 = across(crossed)
    step, come = onward(summed(1, 0, rows) + over_43[:rows].astype(wide))
    second[2] = step = then(second[2], step)
    swap = replica_swap(then(total, step), X_WAYS)
    second.append(ring(second[2]))
    second_twin.append(twin(second[2]))
    come = then(come, step)
    step, come = onward(summed(1, rows, 2 * rows) + over_43[rows:].astype(wide), come)
    got[4] = then(got[4], step)
    crossed = summed(4, 0, 2 * rows).astype(narrow)
    first_3, second[3] = tie([first[3], second[3]], [step, crossed])
    step = jnp.where(core == 0, first_3, second[3])
    last = ring(step)
    second_twin.append(twin(then(second[3], step)))
    total = total + then(swap, step)
    over_2, come, crossed = tie([over_2, come, crossed], [total])
    over_1 = across(crossed)
    step, come = onward(summed(3, 0, 2 * rows) + over_2[: 2 * rows].astype(wide), come)

    def ring_pieces(distance):
        return [
            (first[distance], [(-distance, False, False), (-distance, False, True)]),
            (first_twin[distance], [(distance, False, True), (distance, False, False)]),
            (second[distance], [(-distance, True, False), (-distance, True, True)]),
            (second_twin[distance], [(distance, True, True), (distance, True, False)]),
        ]

    pieces = [
        (own, [(0, False, False)]),
        (own_twin, [(0, False, True)]),
        (side, [(0, True, False)]),
        (side_twin, [(0, True, True)]),
    ]
    earlier = project(
        then(tokens, step), key_cotangent, pieces + ring_pieces(1) + ring_pieces(2), rows
    )
    new_fragment, new_momentum = outer_step(
        then(total, earlier[1]),
        lax.axis_size("replica"),
        kept_rows,
        sign_flips,
        momentum,
        fragment,
    )
    come = then(come, new_momentum)
    step, come = onward(summed(5, 0, 2 * rows) + over_1.astype(wide), come)
    last = then(last, step)
    last_twin = twin(last)
    step = last
    pieces = [
        (last, [(4, "core", False), (4, "core", True)]),
        (last_twin, [(4, "mate", True), (4, "mate", False)]),
    ]
    token_grad, projected = project(
        then(tokens, step), key_cotangent, ring_pieces(2) + ring_pieces(3) + pieces, rows, earlier
    )
    come = then(come, projected)
    rest = twin(come[rows:])
    weight_grad = (
        summed(5, 2 * rows, rows) + over_2[2 * rows :].astype(wide) + come[:rows].astype(wide) + rest.astype(wide)
    ).astype(narrow)[None]
    return (projected, token_grad, weight_grad, new_fragment, new_momentum)


def solution(mesh):
    placed = (
        P(("replica", "fsdp"), None),
        P("replica", "fsdp", None),
        P(("replica", "fsdp"), None),
        P("fsdp", None),
        P("fsdp", None),
        P("replica", "fsdp", None),
        P("fsdp", None),
        P("fsdp", None),
    )
    return jax.shard_map(
        local,
        mesh=mesh,
        in_specs=placed,
        out_specs=(
            P(("replica", "fsdp"), None),
            P(("replica", "fsdp"), None),
            P("replica", "fsdp", None),
            P("fsdp", None),
            P("fsdp", None),
        ),
        check_vma=False,
    )
```
